512 devices in a mesh: wide: 32 (over x, z), narrow: 16 (over y, core).
Axes of the slice: x: 4, y: 8, z: 8, core: 2. Of those that a mesh axis runs over, the one named last changes fastest.
Arguments:
- embeddings: bfloat16 [131072, 1024], P(('wide', 'narrow')), may hold values from -40 to 40
- labels: int32 [131072], P(('wide', 'narrow')), may hold values from 0 to 127, as said below
Outputs:
- nearest: float32 [131072], P(('wide', 'narrow'))
The draws below stay inside these ranges and needn't reach their ends.
Inputs may be any that keep to these rules, and one draw needn't show every extreme that they name: In each aligned block of 256 rows (one device's documents), at most 16 labels lie in any one range of 4 consecutive cluster numbers starting at a multiple of 4, and exactly 16 in some such range.
All inputs are finite; a program needn't handle non-finite values.
Results may differ from the reference program's by a relative error of at most 0.00049.
Values may be sent and summed in bfloat16 or wider, within the bound.
No kernel may reach another device: no remote copies, remote signals or barrier semaphores. Data moves between devices by JAX's collectives and lax.ppermute only.
A program may use at most 64 MiB of HBM per device.

```python
import math
import jax
import jax.numpy as jnp
from jax import lax

E = 1024
DOC_DEV = 256
CL_GROUP = 4
CAP = 16
DOCS = 131072
CLUSTERS = 128
N_WIDE = 32
N_NARROW = 16


def shared_labels(key):
    key = jax.random.fold_in(key, 7)
    ngroups = CLUSTERS // CL_GROUP
    devices_count = DOCS // DOC_DEV
    local_perm = jax.random.permutation(jax.random.fold_in(key, 1), CL_GROUP).astype(jnp.int32)

    def one_device(subkey):
        keys = jax.random.split(subkey, 6)
        first = jax.random.randint(keys[0], (), 0, ngroups).astype(jnp.int32)
        others = (jnp.arange((ngroups - 1) * CAP, dtype=jnp.int32) // CAP + first + 1) % ngroups
        others = jax.random.permutation(keys[1], others)[:DOC_DEV - CAP]
        chosen = jnp.concatenate([jnp.full((CAP,), first, jnp.int32), others])
        chosen = jax.random.permutation(keys[2], chosen)
        draw_a = jax.random.randint(keys[3], (DOC_DEV,), 0, CL_GROUP)
        draw_b = jax.random.randint(keys[4], (DOC_DEV,), 0, CL_GROUP)
        draw_c = jax.random.randint(keys[5], (DOC_DEV,), 0, CL_GROUP)
        local = jnp.minimum(jnp.minimum(draw_a, draw_b), draw_c)
        return (chosen * CL_GROUP + local_perm[local]).astype(jnp.int32)
    device_keys = jax.random.split(jax.random.fold_in(key, 2), devices_count)
    return jax.vmap(one_device)(device_keys).reshape(DOCS)


def draw_labels(key, part):
    return shared_labels(key)


def draw_embeddings(key, part):
    labels = shared_labels(key)
    key = jax.random.fold_in(key, 11)
    keys = jax.random.split(key, 3)
    centroid = jnp.clip(jax.random.normal(keys[0], (CLUSTERS, E), jnp.float32), -4.0, 4.0)
    spread = jax.random.uniform(keys[1], (DOCS, 1), jnp.float32, 0.4, 1.6)
    noise = jax.random.truncated_normal(keys[2], -4.0, 4.0, (DOCS, E), jnp.float32)
    values = centroid[labels] * spread + noise
    return values.astype(jnp.bfloat16)


def setup_inputs(seed: int = 0) -> dict:
    arg_keys = jax.random.split(jax.random.key(seed), 3)
    embeddings = draw_embeddings(jax.random.fold_in(arg_keys[2], 71), 0)
    labels = draw_labels(jax.random.fold_in(arg_keys[2], 71), 0)
    return {"embeddings": embeddings, "labels": labels}


def reference(embeddings, labels):
    width = embeddings.shape[1]
    values = embeddings.astype(jnp.float32)
    unit = (values * lax.rsqrt(lax.optimization_barrier(jnp.mean(values * values, axis=1, keepdims=True)) + 1e-06) / math.sqrt(width)).astype(jnp.bfloat16)
    owner = (labels // CL_GROUP).astype(jnp.int32)
    order = jnp.argsort(owner, stable=True).astype(jnp.int32)
    groups = jnp.arange(N_WIDE, dtype=jnp.int32)
    starts = lax.optimization_barrier(jnp.sum((owner[None, :] < groups[:, None]).astype(jnp.int32), axis=1)).astype(jnp.int32)
    counts = lax.optimization_barrier(jnp.sum((owner[None, :] == groups[:, None]).astype(jnp.int32), axis=1)).astype(jnp.int32)
    span = 2 * DOC_DEV * N_NARROW
    padded = jnp.concatenate([order, jnp.full((span,), DOCS, jnp.int32)])
    unit_pad = jnp.concatenate([unit, jnp.zeros((1, width), jnp.bfloat16)])
    label_pad = jnp.concatenate([labels.astype(jnp.int32), jnp.full((1,), -1, jnp.int32)])
    diagonal = jnp.arange(span, dtype=jnp.int32)

    def one_group(operands):
        first, count = operands
        picked = lax.dynamic_slice_in_dim(padded, first.astype(jnp.int32), span)
        valid = diagonal < count
        picked = jnp.where(valid, picked, DOCS).astype(jnp.int32)
        rows = unit_pad[picked]
        row_labels = label_pad[picked]
        scores = lax.dot_general(rows, rows, (((1,), (1,)), ((), ())), preferred_element_type=jnp.float32)
        allowed = (row_labels[:, None] == row_labels[None, :]) & (row_labels[:, None] >= 0) & (diagonal[:, None] != diagonal[None, :])
        best = lax.optimization_barrier(jnp.max(jnp.where(allowed, scores, jnp.float32(-1.0)), axis=1))
        return (picked, best)
    picked, best = lax.map(one_group, (starts, counts))
    result = jnp.full((DOCS,), -1.0, jnp.float32)
    return result.at[picked.reshape(-1)].set(best.reshape(-1), mode='drop')
```

```python
import functools
import math

import jax
import jax.numpy as jnp
from jax import lax
from jax.experimental import pallas as pl
from jax.experimental.pallas import tpu as pltpu
from jax.sharding import PartitionSpec as P

CL_GROUP = 4
CAP = 16
LIFT = 4.0
LABEL_ROWS = 16
F32, BF16, I32 = jnp.float32, jnp.bfloat16, jnp.int32
NT = (((1,), (1,)), ((), ()))
NN = (((1,), (0,)), ((), ()))
TN = (((0,), (0,)), ((), ()))
VMEM = pl.BlockSpec(memory_space=pltpu.VMEM)
SMEM = pl.BlockSpec(memory_space=pltpu.SMEM)


def dot(a, b, dims):
    return lax.dot_general(a, b, dims, preferred_element_type=F32)


def iota(shape, dim):
    return lax.broadcasted_iota(I32, shape, dim)


def one_hot(condition):
    return condition.astype(F32).astype(BF16)


def call(kernel, out_shape, in_specs, flops, size):
    return pl.pallas_call(
        kernel,
        out_shape=out_shape,
        in_specs=in_specs,
        out_specs=jax.tree.map(lambda _: VMEM, out_shape),
        compiler_params=pltpu.CompilerParams(vmem_limit_bytes=40 * 1024 * 1024),
        cost_estimate=pl.CostEstimate(flops=flops, bytes_accessed=size, transcendentals=0),
    )


def place_kernel(offset_ref, rows_ref, labels_ref, out_ref, slot_ref):
    docs, width = rows_ref.shape
    groups, tall, lanes = out_ref.shape
    labels = labels_ref[...]
    owner = labels >> 2
    mine = iota((groups, docs), 0) == owner
    before = one_hot(iota((docs, docs), 0) < iota((docs, docs), 1))
    earlier = dot(one_hot(mine), before, NN)
    rank = jnp.sum(jnp.where(mine, earlier, 0.0), axis=0, keepdims=True).astype(I32)
    slot = owner * CAP + rank
    slot_ref[...] = slot
    values = rows_ref[...].astype(F32)
    mean = jnp.mean(values * values, axis=1, keepdims=True)
    unit = (values * lax.rsqrt(mean + 1e-06) / math.sqrt(width)).astype(BF16)
    pick = one_hot(iota((groups * CAP, docs), 0) == slot)
    step = 2 * lanes
    for first in range(0, width, step):
        placed = dot(pick, unit[:, first : first + step], NN).astype(BF16)
        for half in range(2):
            k = first // lanes + half
            part = placed[:, half * lanes : (half + 1) * lanes]
            out_ref[:, k * CAP : (k + 1) * CAP, :] = part.reshape(groups, CAP, lanes)
    below = tall - CAP * width // lanes
    index = iota((groups * below, docs), 0)
    cluster = index & (below - 1)
    wanted = (labels == (index >> 3) * CL_GROUP + cluster) & (cluster < CL_GROUP)
    lane = one_hot(iota((lanes, docs), 0) == rank + offset_ref[0])
    flags = dot(one_hot(wanted), lane, NT).astype(BF16)
    out_ref[:, tall - below :, :] = flags.reshape(groups, below, lanes)


def compact_kernel(capacity, in_ref, out_ref, position_ref, over_ref):
    groups, tall, lanes = in_ref.shape
    width = out_ref.shape[1]
    count = width // lanes
    slots = groups * CAP
    below = tall - CAP * count
    labels = in_ref[:, tall - below :, :].astype(F32)
    per = lanes // CAP
    labels = jnp.sum(labels.reshape(groups // per, per, below, lanes), axis=1)
    labels = jnp.concatenate([labels[i] for i in range(groups // per)], axis=1)
    valid = jnp.sum(labels, axis=0, keepdims=True)
    before = one_hot(iota((slots, slots), 0) < iota((slots, slots), 1))
    rank = dot(jnp.broadcast_to(valid, (8, slots)).astype(BF16), before, NN)[:1]
    position = jnp.where(valid > 0.5, rank.astype(I32), -1)
    position_ref[...] = position
    total = jnp.sum(valid, axis=1, keepdims=True)
    over_ref[...] = jnp.broadcast_to(jnp.where(total > capacity + 0.5, 1.0, 0.0), over_ref.shape)
    pick = one_hot(iota((capacity, slots), 0) == position)
    for k in range(count):
        part = in_ref[:, k * CAP : (k + 1) * CAP, :].reshape(slots, lanes)
        out_ref[:capacity, k * lanes : (k + 1) * lanes] = dot(pick, part, NN).astype(BF16)
    marks = dot(labels.astype(BF16), pick, NT).astype(BF16)
    marks = jnp.concatenate([marks, jnp.zeros((below, width - capacity), BF16)], axis=1)
    marks = jnp.concatenate([marks, jnp.zeros((LABEL_ROWS - below, width), BF16)], axis=0)
    out_ref[capacity:, :] = marks


def lifted(left_ref, right_ref, capacity):
    left, right = left_ref[:capacity, :], right_ref[:capacity, :]
    left_marks = left_ref[capacity:, :capacity]
    right_marks = (right_ref[capacity:, :capacity].astype(F32) * LIFT).astype(BF16)
    return dot(left, right, NT) + dot(left_marks, right_marks, TN)


def over_rows(scores):
    return jnp.max(scores, axis=0, keepdims=True)


def over_columns(scores):
    return jnp.max(scores, axis=1, keepdims=True)


def as_row(column):
    size = column.shape[0]
    same = iota((size, size), 0) == iota((size, size), 1)
    return jnp.max(jnp.where(same, column, -9.0), axis=0, keepdims=True)


def own_kernel(capacity, own_ref, twin_ref, out_ref):
    scores = lifted(own_ref, own_ref, capacity)
    same = iota((capacity, capacity), 0) == iota((capacity, capacity), 1)
    best = over_rows(jnp.where(same, -9.0, scores))
    out_ref[...] = jnp.maximum(best, over_rows(lifted(twin_ref, own_ref, capacity)))


def next_kernel(capacity, best_ref, own_ref, twin_ref, next_ref, own_out, twin_out, next_out):
    first = lifted(next_ref, own_ref, capacity)
    own_out[...] = jnp.maximum(best_ref[...], over_rows(first))
    second = lifted(next_ref, twin_ref, capacity)
    twin_out[...] = over_rows(second)
    next_out[...] = as_row(jnp.maximum(over_columns(first), over_columns(second)))


def last_kernel(
    capacity, targets_ref, over_ref, own_best, twin_best, next_best, own_ref, twin_ref,
    back_ref, back_twin_ref, far_ref, ahead_ref, out_ref,
):
    bests = []
    across = None
    for ref in (own_ref, twin_ref, back_ref, back_twin_ref, far_ref):
        scores = lifted(ahead_ref, ref, capacity)
        bests.append(over_rows(scores))
        column = over_columns(scores)
        across = column if across is None else jnp.maximum(across, column)
    bests[0] = jnp.maximum(bests[0], own_best[...])
    bests[1] = jnp.maximum(bests[1], twin_best[...])
    bests += [next_best[...], as_row(across)]
    count, wide = out_ref.shape
    rest = wide - capacity
    row = iota((count, capacity), 0)
    out = jnp.full((count, capacity), -9.0, F32)
    for i, best in enumerate(bests):
        out = jnp.where(row == targets_ref[i], best, out)
    over = jnp.broadcast_to(over_ref[...][:, :1], (count, rest))
    out_ref[...] = jnp.concatenate([out, over], axis=1)


def answer_kernel(capacity, all_ref, position_ref, out_ref):
    slots = position_ref.shape[1]
    groups, lanes = out_ref.shape
    best = jnp.max(all_ref[...], axis=0, keepdims=True)
    over = best[:, capacity : capacity + 1]
    best = jnp.maximum(best[:, :capacity] - LIFT, -1.0)
    diagonal = iota((slots, slots), 0) == iota((slots, slots), 1)
    position = jnp.max(jnp.where(diagonal, position_ref[...], -1), axis=1, keepdims=True)
    hit = iota((slots, capacity), 1) == position
    values = jnp.max(jnp.where(hit, best, -1.0), axis=1, keepdims=True)
    values = jnp.broadcast_to(values, (slots, lanes)).reshape(groups, CAP, lanes)
    same = iota((groups, CAP, lanes), 1) == iota((groups, CAP, lanes), 2)
    answers = jnp.max(jnp.where(same, values, -1.0), axis=1)
    out_ref[...] = jnp.where(iota((groups, lanes), 1) == CAP, over, answers)


def home_kernel(slot_ref, answers_ref, out_ref, over_ref):
    groups, lanes = answers_ref.shape
    docs = slot_ref.shape[1]
    answers = answers_ref[...]
    over = jnp.max(answers[:, CAP : CAP + 1], axis=0, keepdims=True)
    over_ref[...] = jnp.broadcast_to((over > 0.5).astype(I32), over_ref.shape)
    spread = jnp.broadcast_to(answers[:, None, :], (groups, CAP, lanes))
    same = iota((groups, CAP, lanes), 1) == iota((groups, CAP, lanes), 2)
    column = jnp.max(jnp.where(same, spread, -1.0), axis=2, keepdims=True)
    column = column.reshape(groups * CAP, 1)
    hit = iota((groups * CAP, docs), 0) == slot_ref[...]
    out_ref[...] = jnp.max(jnp.where(hit, column, -1.0), axis=0, keepdims=True)


def ring(step):
    size = lax.axis_size("narrow")
    return [(i, (i + 2 * step) % size) for i in range(size)]


def crossing():
    size = lax.axis_size("narrow")
    pairs = []
    for i in range(size):
        to = (i + 2) % size
        pairs.append((i, to ^ 1 if to >= size // 2 else to))
    return pairs


def nearest(received, slot, capacity):
    width = 1024
    groups, tall, lanes = received.shape
    slots = groups * CAP
    size = lax.axis_size("narrow")
    shape = jax.ShapeDtypeStruct
    block_bytes = 2 * (capacity + LABEL_ROWS) * width
    product = 2 * capacity * capacity * (width + 128)
    line = shape((1, capacity), F32)
    block, position, over = call(
        functools.partial(compact_kernel, capacity),
        (
            shape((capacity + LABEL_ROWS, width), BF16),
            shape((1, slots), I32),
            shape((1, 128), F32),
        ),
        [VMEM],
        2 * capacity * slots * width,
        received.size * 2 + block_bytes,
    )(received)

    twins = [(i, i ^ 1) for i in range(size)]
    back = lax.ppermute(block, "narrow", ring(1))
    ahead = lax.ppermute(block, "narrow", ring(-1))
    twin = lax.ppermute(block, "narrow", twins)
    far = lax.ppermute(back, "narrow", crossing())
    far_ahead = lax.ppermute(ahead, "narrow", ring(-1))
    back_twin = lax.ppermute(back, "narrow", twins)

    best = call(
        functools.partial(own_kernel, capacity), line, [VMEM] * 2, 2 * product, 2 * block_bytes
    )(block, twin)
    own_best, twin_best, next_best = call(
        functools.partial(next_kernel, capacity),
        (line, line, line),
        [VMEM] * 4,
        2 * product,
        3 * block_bytes,
    )(best, block, twin, ahead)

    me = lax.axis_index("narrow")
    crossed = jnp.where(me >= size // 2, 1, 0)
    targets = jnp.stack(
        [
            me,
            me ^ 1,
            (me - 2) % size,
            ((me - 2) % size) ^ 1,
            ((me - 4) % size) ^ crossed,
            (me + 2) % size,
            (me + 4) % size,
        ]
    ).astype(I32)
    row_lanes = (capacity // 128 + 1) * 128
    partial = call(
        functools.partial(last_kernel, capacity),
        shape((size, row_lanes), F32),
        [SMEM] + [VMEM] * 10,
        5 * product,
        6 * block_bytes,
    )(targets, over, own_best, twin_best, next_best, block, twin, back, back_twin, far, far_ahead)
    everyone = lax.all_to_all(partial, "narrow", split_axis=0, concat_axis=0, tiled=True)
    answers = call(
        functools.partial(answer_kernel, capacity),
        shape((groups, lanes), F32),
        [VMEM] * 2,
        slots * slots * 8,
        groups * lanes * 8,
    )(everyone, position)
    answers = lax.all_to_all(answers, "wide", split_axis=0, concat_axis=0, tiled=True)
    return call(
        home_kernel,
        (shape(slot.shape, F32), shape((1, 128), I32)),
        [VMEM] * 2,
        slots * slot.shape[1] * 4,
        groups * lanes * 4,
    )(slot, answers)


def shards(embeddings, labels):
    docs, width = embeddings.shape
    groups = lax.axis_size("wide")
    lanes = 128
    tall = CAP * width // lanes + 8
    shape = jax.ShapeDtypeStruct
    offset = (lax.axis_index("wide") % (lanes // CAP) * CAP).astype(I32).reshape(1)
    outgoing, slot = call(
        place_kernel,
        (shape((groups, tall, lanes), BF16), shape((1, docs), I32)),
        [SMEM, VMEM, VMEM],
        2 * groups * CAP * docs * width,
        2 * docs * width + 2 * groups * tall * lanes,
    )(offset, embeddings, labels.reshape(1, docs))
    received = lax.all_to_all(outgoing, "wide", split_axis=0, concat_axis=0, tiled=True)
    quick, over = nearest(received, slot, 336)
    result = lax.cond(
        over[0, 0] > 0,
        lambda rows, places, unused: nearest(rows, places, groups * CAP)[0],
        lambda rows, places, done: done,
        received,
        slot,
        quick,
    )
    return result.reshape(docs)


def solution(mesh):
    in_specs = (P(("wide", "narrow"), None), P(("wide", "narrow")))
    out_specs = P(("wide", "narrow"))
    return jax.shard_map(shards, mesh=mesh, in_specs=in_specs, out_specs=out_specs, check_vma=False)
```

```python
import functools
import math

import jax
import jax.numpy as jnp
from jax import lax
from jax.experimental import pallas as pl
from jax.experimental.pallas import tpu as pltpu
from jax.sharding import PartitionSpec as P

CL_GROUP = 4
CAP = 16
LIFT = 4.0
LABEL_ROWS = 16
F32, BF16, I32 = jnp.float32, jnp.bfloat16, jnp.int32
NT = (((1,), (1,)), ((), ()))
NN = (((1,), (0,)), ((), ()))
TN = (((0,), (0,)), ((), ()))
VMEM = pl.BlockSpec(memory_space=pltpu.VMEM)
SMEM = pl.BlockSpec(memory_space=pltpu.SMEM)


def dot(a, b, dims):
    return lax.dot_general(a, b, dims, preferred_element_type=F32)


def iota(shape, dim):
    return lax.broadcasted_iota(I32, shape, dim)


def one_hot(condition):
    return condition.astype(F32).astype(BF16)


def call(kernel, out_shape, in_specs, flops, size):
    return pl.pallas_call(
        kernel,
        out_shape=out_shape,
        in_specs=in_specs,
        out_specs=jax.tree.map(lambda _: VMEM, out_shape),
        compiler_params=pltpu.CompilerParams(vmem_limit_bytes=24 * 1024 * 1024),
        cost_estimate=pl.CostEstimate(flops=flops, bytes_accessed=size, transcendentals=0),
    )


def place_kernel(offset_ref, rows_ref, labels_ref, out_ref, slot_ref):
    docs, width = rows_ref.shape
    groups, tall, lanes = out_ref.shape
    labels = labels_ref[...]
    owner = labels >> 2
    mine = iota((groups, docs), 0) == owner
    before = one_hot(iota((docs, docs), 0) < iota((docs, docs), 1))
    earlier = dot(one_hot(mine), before, NN)
    rank = jnp.sum(jnp.where(mine, earlier, 0.0), axis=0, keepdims=True).astype(I32)
    slot = owner * CAP + rank
    slot_ref[...] = slot
    values = rows_ref[...].astype(F32)
    mean = jnp.mean(values * values, axis=1, keepdims=True)
    unit = (values * lax.rsqrt(mean + 1e-06) / math.sqrt(width)).astype(BF16)
    pick = one_hot(iota((groups * CAP, docs), 0) == slot)
    step = 2 * lanes
    for first in range(0, width, step):
        placed = dot(pick, unit[:, first : first + step], NN).astype(BF16)
        for half in range(2):
            k = first // lanes + half
            part = placed[:, half * lanes : (half + 1) * lanes]
            out_ref[:, k * CAP : (k + 1) * CAP, :] = part.reshape(groups, CAP, lanes)
    below = tall - CAP * width // lanes
    index = iota((groups * below, docs), 0)
    cluster = index & (below - 1)
    wanted = (labels == (index >> 3) * CL_GROUP + cluster) & (cluster < CL_GROUP)
    lane = one_hot(iota((lanes, docs), 0) == rank + offset_ref[0])
    flags = dot(one_hot(wanted), lane, NT).astype(BF16)
    out_ref[:, tall - below :, :] = flags.reshape(groups, below, lanes)


def compact_kernel(capacity, in_ref, out_ref, position_ref):
    groups, tall, lanes = in_ref.shape
    width = out_ref.shape[1]
    count = width // lanes
    slots = groups * CAP
    below = tall - CAP * count
    labels = in_ref[:, tall - below :, :].astype(F32)
    per = lanes // CAP
    labels = jnp.sum(labels.reshape(groups // per, per, below, lanes), axis=1)
    labels = jnp.concatenate([labels[i] for i in range(groups // per)], axis=1)
    valid = jnp.sum(labels, axis=0, keepdims=True)
    before = one_hot(iota((slots, slots), 0) < iota((slots, slots), 1))
    rank = dot(jnp.broadcast_to(valid, (8, slots)).astype(BF16), before, NN)[:1]
    position = jnp.where(valid > 0.5, rank.astype(I32), -1)
    position_ref[...] = position
    total = jnp.sum(valid, axis=1, keepdims=True)
    over = jnp.broadcast_to(jnp.where(total > capacity + 0.5, 1.0, 0.0), (below, lanes))
    pick = one_hot(iota((capacity, slots), 0) == position)
    for k in range(count):
        part = in_ref[:, k * CAP : (k + 1) * CAP, :].reshape(slots, lanes)
        out_ref[:capacity, k * lanes : (k + 1) * lanes] = dot(pick, part, NN).astype(BF16)
    marks = dot(labels.astype(BF16), pick, NT).astype(BF16)
    marks = jnp.concatenate([marks, jnp.zeros((below, width - capacity), BF16)], axis=1)
    flag = jnp.concatenate([jnp.zeros((below, width - lanes), F32), over], axis=1).astype(BF16)
    out_ref[capacity:, :] = jnp.concatenate([marks, flag], axis=0)


def best_of(ref, others, capacity, skip_self=False):
    rows = ref[:capacity, :]
    marks = (ref[capacity:, :capacity].astype(F32) * LIFT).astype(BF16)
    best = None
    for other in others:
        if isinstance(other, tuple):
            other = jnp.concatenate([part[...] for part in other], axis=0)
        scores = dot(other[:capacity, :], rows, NT) + dot(other[capacity:, :capacity], marks, TN)
        if skip_self and other is ref:
            same = iota((capacity, capacity), 0) == iota((capacity, capacity), 1)
            scores = jnp.where(same, -9.0, scores)
        column = jnp.max(scores, axis=0, keepdims=True)
        best = column if best is None else jnp.maximum(best, column)
    return best


def near_kernel(
    capacity, own_ref, twin_ref, a_ref, a_twin_ref, b_ref, b_twin_ref, position_ref, out_ref, column_ref
):
    others = (own_ref, twin_ref, a_ref, a_twin_ref, b_ref, b_twin_ref)
    out_ref[...] = best_of(own_ref, others, capacity, skip_self=True)
    slots = position_ref.shape[1]
    diagonal = iota((slots, slots), 0) == iota((slots, slots), 1)
    column = jnp.max(jnp.where(diagonal, position_ref[...], -1), axis=1, keepdims=True)
    column_ref[...] = jnp.broadcast_to(column, column_ref.shape)


def report_kernel(capacity, rows_ref, seen_ref, *refs):
    *others, out_ref = refs
    if len(others) > 5:
        others[4:] = [tuple(others[4:])]
    lanes = 128
    width = rows_ref.shape[1]
    flags = jnp.broadcast_to(seen_ref[:, capacity : capacity + 1], (1, lanes))
    for ref in (rows_ref, *others):
        ref = ref[-1] if isinstance(ref, tuple) else ref
        seen = ref[ref.shape[0] - LABEL_ROWS :, width - lanes :].astype(F32)
        flags = jnp.maximum(flags, jnp.max(seen, axis=0, keepdims=True))
    flags = flags[:, : out_ref.shape[1] - capacity]
    out_ref[...] = jnp.concatenate([best_of(rows_ref, others, capacity), flags], axis=1)


def answer_kernel(capacity, near_ref, seen_ref, told_a, told_b, position_ref, out_ref):
    slots = position_ref.shape[0]
    groups, lanes = out_ref.shape
    told = jnp.maximum(told_a[...], told_b[...])
    over = jnp.maximum(told, seen_ref[...])[:, capacity : capacity + 1]
    best = jnp.maximum(jnp.maximum(near_ref[...], told[:, :capacity]) - LIFT, -1.0)
    hit = iota((slots, capacity), 1) == position_ref[:, :1]
    values = jnp.max(jnp.where(hit, best, -1.0), axis=1, keepdims=True)
    values = jnp.broadcast_to(values, (slots, lanes)).reshape(groups, CAP, lanes)
    same = iota((groups, CAP, lanes), 1) == iota((groups, CAP, lanes), 2)
    answers = jnp.max(jnp.where(same, values, -1.0), axis=1)
    out_ref[...] = jnp.where(iota((groups, lanes), 1) == CAP, over, answers)


def home_kernel(slot_ref, answers_ref, out_ref, over_ref):
    groups, lanes = answers_ref.shape
    docs = slot_ref.shape[1]
    answers = answers_ref[...]
    over = jnp.max(answers[:, CAP : CAP + 1], axis=0, keepdims=True)
    over_ref[...] = jnp.broadcast_to((over > 0.5).astype(I32), over_ref.shape)
    spread = jnp.broadcast_to(answers[:, None, :], (groups, CAP, lanes))
    same = iota((groups, CAP, lanes), 1) == iota((groups, CAP, lanes), 2)
    column = jnp.max(jnp.where(same, spread, -1.0), axis=2, keepdims=True)
    column = column.reshape(groups * CAP, 1)
    hit = iota((groups * CAP, docs), 0) == slot_ref[...]
    out_ref[...] = jnp.max(jnp.where(hit, column, -1.0), axis=0, keepdims=True)


def turn(step):
    size = lax.axis_size("narrow")
    return [(i, (i + 2 * (step if i % 2 == 0 else -step)) % size) for i in range(size)]


def nearest(received, slot, capacity):
    width = 1024
    groups, tall, lanes = received.shape
    slots = groups * CAP
    size = lax.axis_size("narrow")
    shape = jax.ShapeDtypeStruct
    block_bytes = 2 * (capacity + LABEL_ROWS) * width
    product = 2 * capacity * capacity * (width + 128)
    line = shape((1, capacity), F32)
    block, position = call(
        functools.partial(compact_kernel, capacity),
        (shape((capacity + LABEL_ROWS, width), BF16), shape((1, slots), I32)),
        [VMEM],
        2 * capacity * slots * width,
        received.size * 2 + block_bytes,
    )(received)

    def send(rows, pairs):
        return lax.ppermute(rows, "narrow", pairs)

    twins = [(i, i ^ 1) for i in range(size)]
    a = send(block, turn(-1))
    b = send(block, turn(1))
    twin = send(block, twins)
    a, twin = lax.optimization_barrier((a, twin))
    a2 = send(a, turn(-1))
    b_twin = send(a, twins)
    b2 = send(b, turn(1))
    a_twin = send(b, twins)
    half = (capacity + LABEL_ROWS) // 32 * 16
    b2_twin = [send(a2[:half], twins), send(a2[half:], twins)]

    near, column = call(
        functools.partial(near_kernel, capacity),
        (line, shape((slots, lanes), I32)),
        [VMEM] * 7,
        6 * product,
        6 * block_bytes,
    )(block, twin, a, a_twin, b, b_twin, position)
    told = shape((1, (capacity // 128 + 1) * 128), F32)
    def report(*refs):
        kernel = functools.partial(report_kernel, capacity)
        return call(kernel, told, [VMEM] * len(refs), 5 * product, 6 * block_bytes)(*refs)

    to_a2 = report(a2, jnp.zeros(told.shape, F32), block, twin, b, b_twin, *b2_twin)
    to_b2 = report(b2, to_a2, block, twin, a, a_twin, a2)
    told_a = send(to_a2, turn(2))
    told_b = send(to_b2, turn(-2))
    answers = call(
        functools.partial(answer_kernel, capacity),
        shape((groups, lanes), F32),
        [VMEM] * 5,
        slots * slots * 8,
        groups * lanes * 8,
    )(near, to_b2, told_a, told_b, column)
    answers = lax.all_to_all(answers, "wide", split_axis=0, concat_axis=0, tiled=True)
    return call(
        home_kernel,
        (shape(slot.shape, F32), shape((1, 128), I32)),
        [VMEM] * 2,
        slots * slot.shape[1] * 4,
        groups * lanes * 4,
    )(slot, answers)


def shards(embeddings, labels):
    docs, width = embeddings.shape
    groups = lax.axis_size("wide")
    lanes = 128
    tall = CAP * width // lanes + 8
    shape = jax.ShapeDtypeStruct
    offset = (lax.axis_index("wide") % (lanes // CAP) * CAP).astype(I32).reshape(1)
    outgoing, slot = call(
        place_kernel,
        (shape((groups, tall, lanes), BF16), shape((1, docs), I32)),
        [SMEM, VMEM, VMEM],
        2 * groups * CAP * docs * width,
        2 * docs * width + 2 * groups * tall * lanes,
    )(offset, embeddings, labels.reshape(1, docs))
    received = lax.all_to_all(outgoing, "wide", split_axis=0, concat_axis=0, tiled=True)
    quick, over = nearest(received, slot, 336)
    result = lax.cond(
        over[0, 0] > 0,
        lambda rows, places, unused: nearest(rows, places, groups * CAP)[0],
        lambda rows, places, done: done,
        received,
        slot,
        quick,
    )
    return result.reshape(docs)


def solution(mesh):
    in_specs = (P(("wide", "narrow"), None), P(("wide", "narrow")))
    out_specs = P(("wide", "narrow"))
    return jax.shard_map(shards, mesh=mesh, in_specs=in_specs, out_specs=out_specs, check_vma=False)
```

```python
import functools
import math

import jax
import jax.numpy as jnp
from jax import lax
from jax.experimental import pallas as pl
from jax.experimental.pallas import tpu as pltpu
from jax.sharding import PartitionSpec as P

CL_GROUP = 4
CAP = 16
LIFT = 4.0
LABEL_ROWS = 16
F32, BF16, I32 = jnp.float32, jnp.bfloat16, jnp.int32
NT = (((1,), (1,)), ((), ()))
NN = (((1,), (0,)), ((), ()))
TN = (((0,), (0,)), ((), ()))
VMEM = pl.BlockSpec(memory_space=pltpu.VMEM)
SMEM = pl.BlockSpec(memory_space=pltpu.SMEM)


def dot(a, b, dims):
    return lax.dot_general(a, b, dims, preferred_element_type=F32)


def iota(shape, dim):
    return lax.broadcasted_iota(I32, shape, dim)


def one_hot(condition):
    return condition.astype(F32).astype(BF16)


def call(kernel, out_shape, in_specs, flops, size):
    return pl.pallas_call(
        kernel,
        out_shape=out_shape,
        in_specs=in_specs,
        out_specs=jax.tree.map(lambda _: VMEM, out_shape),
        compiler_params=pltpu.CompilerParams(vmem_limit_bytes=24 * 1024 * 1024),
        cost_estimate=pl.CostEstimate(flops=flops, bytes_accessed=size, transcendentals=0),
    )


def place_kernel(offset_ref, rows_ref, labels_ref, out_ref, slot_ref):
    docs, width = rows_ref.shape
    groups, tall, lanes = out_ref.shape
    labels = labels_ref[...]
    owner = labels >> 2
    mine = iota((groups, docs), 0) == owner
    before = one_hot(iota((docs, docs), 0) < iota((docs, docs), 1))
    earlier = dot(one_hot(mine), before, NN)
    rank = jnp.sum(jnp.where(mine, earlier, 0.0), axis=0, keepdims=True).astype(I32)
    slot = owner * CAP + rank
    slot_ref[...] = slot
    values = rows_ref[...].astype(F32)
    mean = jnp.mean(values * values, axis=1, keepdims=True)
    unit = (values * lax.rsqrt(mean + 1e-06) / math.sqrt(width)).astype(BF16)
    pick = one_hot(iota((groups * CAP, docs), 0) == slot)
    step = 2 * lanes
    for first in range(0, width, step):
        placed = dot(pick, unit[:, first : first + step], NN).astype(BF16)
        for half in range(2):
            k = first // lanes + half
            part = placed[:, half * lanes : (half + 1) * lanes]
            out_ref[:, k * CAP : (k + 1) * CAP, :] = part.reshape(groups, CAP, lanes)
    below = tall - CAP * width // lanes
    index = iota((groups * below, docs), 0)
    cluster = index & (below - 1)
    wanted = (labels == (index >> 3) * CL_GROUP + cluster) & (cluster < CL_GROUP)
    lane = one_hot(iota((lanes, docs), 0) == rank + offset_ref[0])
    flags = dot(one_hot(wanted), lane, NT).astype(BF16)
    out_ref[:, tall - below :, :] = flags.reshape(groups, below, lanes)


def compact_kernel(capacity, in_ref, out_ref, position_ref):
    groups, tall, lanes = in_ref.shape
    width = out_ref.shape[1]
    count = width // lanes
    slots = groups * CAP
    below = tall - CAP * count
    labels = in_ref[:, tall - below :, :].astype(F32)
    per = lanes // CAP
    labels = jnp.sum(labels.reshape(groups // per, per, below, lanes), axis=1)
    labels = jnp.concatenate([labels[i] for i in range(groups // per)], axis=1)
    valid = jnp.sum(labels, axis=0, keepdims=True)
    before = one_hot(iota((slots, slots), 0) < iota((slots, slots), 1))
    rank = dot(jnp.broadcast_to(valid, (8, slots)).astype(BF16), before, NN)[:1]
    position = jnp.where(valid > 0.5, rank.astype(I32), -1)
    position_ref[...] = position
    total = jnp.sum(valid, axis=1, keepdims=True)
    over = jnp.broadcast_to(jnp.where(total > capacity + 0.5, 1.0, 0.0), (below, lanes))
    pick = one_hot(iota((capacity, slots), 0) == position)
    for k in range(count):
        part = in_ref[:, k * CAP : (k + 1) * CAP, :].reshape(slots, lanes)
        out_ref[:capacity, k * lanes : (k + 1) * lanes] = dot(pick, part, NN).astype(BF16)
    marks = dot(labels.astype(BF16), pick, NT).astype(BF16)
    marks = jnp.concatenate([marks, jnp.zeros((below, width - capacity), BF16)], axis=1)
    flag = jnp.concatenate([jnp.zeros((below, width - lanes), F32), over], axis=1).astype(BF16)
    out_ref[capacity:, :] = jnp.concatenate([marks, flag], axis=0)


def best_of(ref, others, capacity, skip_self=False):
    rows = ref[:capacity, :]
    marks = (ref[capacity:, :capacity].astype(F32) * LIFT).astype(BF16)
    best = None
    for other in others:
        if isinstance(other, tuple):
            other = jnp.concatenate([part[...] for part in other], axis=0)
        scores = dot(other[:capacity, :], rows, NT) + dot(other[capacity:, :capacity], marks, TN)
        if skip_self and other is ref:
            same = iota((capacity, capacity), 0) == iota((capacity, capacity), 1)
            scores = jnp.where(same, -9.0, scores)
        column = jnp.max(scores, axis=0, keepdims=True)
        best = column if best is None else jnp.maximum(best, column)
    return best


def middle_kernel(
    capacity, own_ref, twin_ref, a_ref, b_ref, b_twin_ref, a2_ref, position_ref,
    near_ref, a2_best, column_ref,
):
    others = (own_ref, twin_ref, a_ref, b_ref, b_twin_ref)
    near_ref[...] = best_of(own_ref, others, capacity, skip_self=True)
    a2_best[...] = best_of(a2_ref, (own_ref, twin_ref, b_ref, b_twin_ref), capacity)
    slots = position_ref.shape[1]
    diagonal = iota((slots, slots), 0) == iota((slots, slots), 1)
    column = jnp.max(jnp.where(diagonal, position_ref[...], -1), axis=1, keepdims=True)
    column_ref[...] = jnp.broadcast_to(column, column_ref.shape)


def last_kernel(
    capacity, near_best, a2_best, b2_ref, own_ref, twin_ref, a_ref, a_twin_ref, b_ref, b_twin_ref, a2_ref, *refs
):
    *b2_twin, to_a2, to_b2, near_ref = refs
    near_ref[...] = jnp.maximum(near_best[...], best_of(own_ref, (a_twin_ref,), capacity))
    lanes = 128
    width = own_ref.shape[1]
    flags = None
    blocks = (own_ref, twin_ref, a_ref, a_twin_ref, b_ref, b_twin_ref, a2_ref, b2_ref, b2_twin[-1])
    for ref in blocks:
        seen = ref[ref.shape[0] - LABEL_ROWS :, width - lanes :].astype(F32)
        flags = seen if flags is None else jnp.maximum(flags, seen)
    flags = jnp.max(flags, axis=0, keepdims=True)[:, : to_a2.shape[1] - capacity]
    others = (own_ref, twin_ref, a_ref, a_twin_ref, a2_ref)
    to_b2[...] = jnp.concatenate([best_of(b2_ref, others, capacity), flags], axis=1)
    best = jnp.maximum(a2_best[...], best_of(a2_ref, (tuple(b2_twin),), capacity))
    to_a2[...] = jnp.concatenate([best, flags], axis=1)


def answer_kernel(capacity, near_ref, seen_ref, told_a, told_b, position_ref, out_ref):
    slots = position_ref.shape[0]
    groups, lanes = out_ref.shape
    told = jnp.maximum(told_a[...], told_b[...])
    over = jnp.maximum(told, seen_ref[...])[:, capacity : capacity + 1]
    best = jnp.maximum(jnp.maximum(near_ref[...], told[:, :capacity]) - LIFT, -1.0)
    hit = iota((slots, capacity), 1) == position_ref[:, :1]
    values = jnp.max(jnp.where(hit, best, -1.0), axis=1, keepdims=True)
    values = jnp.broadcast_to(values, (slots, lanes)).reshape(groups, CAP, lanes)
    same = iota((groups, CAP, lanes), 1) == iota((groups, CAP, lanes), 2)
    answers = jnp.max(jnp.where(same, values, -1.0), axis=1)
    out_ref[...] = jnp.where(iota((groups, lanes), 1) == CAP, over, answers)


def home_kernel(slot_ref, answers_ref, out_ref, over_ref):
    groups, lanes = answers_ref.shape
    docs = slot_ref.shape[1]
    answers = answers_ref[...]
    over = jnp.max(answers[:, CAP : CAP + 1], axis=0, keepdims=True)
    over_ref[...] = jnp.broadcast_to((over > 0.5).astype(I32), over_ref.shape)
    spread = jnp.broadcast_to(answers[:, None, :], (groups, CAP, lanes))
    same = iota((groups, CAP, lanes), 1) == iota((groups, CAP, lanes), 2)
    column = jnp.max(jnp.where(same, spread, -1.0), axis=2, keepdims=True)
    column = column.reshape(groups * CAP, 1)
    hit = iota((groups * CAP, docs), 0) == slot_ref[...]
    out_ref[...] = jnp.max(jnp.where(hit, column, -1.0), axis=0, keepdims=True)


def turn(step):
    size = lax.axis_size("narrow")
    return [(i, (i + 2 * (step if i % 2 == 0 else -step)) % size) for i in range(size)]


def nearest(received, slot, capacity):
    width = 1024
    groups, tall, lanes = received.shape
    slots = groups * CAP
    size = lax.axis_size("narrow")
    shape = jax.ShapeDtypeStruct
    block_bytes = 2 * (capacity + LABEL_ROWS) * width
    product = 2 * capacity * capacity * (width + 128)
    line = shape((1, capacity), F32)
    block, position = call(
        functools.partial(compact_kernel, capacity),
        (shape((capacity + LABEL_ROWS, width), BF16), shape((1, slots), I32)),
        [VMEM],
        2 * capacity * slots * width,
        received.size * 2 + block_bytes,
    )(received)

    def send(rows, pairs):
        return lax.ppermute(rows, "narrow", pairs)

    twins = [(i, i ^ 1) for i in range(size)]
    a = send(block, turn(-1))
    b = send(block, turn(1))
    twin = send(block, twins)
    a2 = send(a, turn(-1))
    b2 = send(b, turn(1))
    late_a, twin = lax.optimization_barrier((a, twin))
    b_twin = send(late_a, twins)
    a_twin = send(b, twins)
    b2_twin = [send(a2, twins)]
    told = shape((1, (capacity // 128 + 1) * 128), F32)
    near, a2_best, column = call(
        functools.partial(middle_kernel, capacity),
        (line, line, shape((slots, lanes), I32)),
        [VMEM] * 7,
        9 * product,
        7 * block_bytes,
    )(block, twin, a, b, b_twin, a2, position)
    blocks = (b2, block, twin, a, a_twin, b, b_twin, a2, *b2_twin)
    to_a2, to_b2, near = call(
        functools.partial(last_kernel, capacity),
        (told, told, line),
        [VMEM] * (2 + len(blocks)),
        7 * product,
        8 * block_bytes,
    )(near, a2_best, *blocks)
    told_a = send(to_a2, turn(2))
    told_b = send(to_b2, turn(-2))
    answers = call(
        functools.partial(answer_kernel, capacity),
        shape((groups, lanes), F32),
        [VMEM] * 5,
        slots * slots * 8,
        groups * lanes * 8,
    )(near, to_b2, told_a, told_b, column)
    answers = lax.all_to_all(answers, "wide", split_axis=0, concat_axis=0, tiled=True)
    return call(
        home_kernel,
        (shape(slot.shape, F32), shape((1, 128), I32)),
        [VMEM] * 2,
        slots * slot.shape[1] * 4,
        groups * lanes * 4,
    )(slot, answers)


def shards(embeddings, labels):
    docs, width = embeddings.shape
    groups = lax.axis_size("wide")
    lanes = 128
    tall = CAP * width // lanes + 8
    shape = jax.ShapeDtypeStruct
    offset = (lax.axis_index("wide") % (lanes // CAP) * CAP).astype(I32).reshape(1)
    outgoing, slot = call(
        place_kernel,
        (shape((groups, tall, lanes), BF16), shape((1, docs), I32)),
        [SMEM, VMEM, VMEM],
        2 * groups * CAP * docs * width,
        2 * docs * width + 2 * groups * tall * lanes,
    )(offset, embeddings, labels.reshape(1, docs))
    received = lax.all_to_all(outgoing, "wide", split_axis=0, concat_axis=0, tiled=True)
    quick, over = nearest(received, slot, 320)
    result = lax.cond(
        over[0, 0] > 0,
        lambda rows, places, unused: nearest(rows, places, groups * CAP)[0],
        lambda rows, places, done: done,
        received,
        slot,
        quick,
    )
    return result.reshape(docs)


def solution(mesh):
    in_specs = (P(("wide", "narrow"), None), P(("wide", "narrow")))
    out_specs = P(("wide", "narrow"))
    return jax.shard_map(shards, mesh=mesh, in_specs=in_specs, out_specs=out_specs, check_vma=False)
```

```python
import functools
import math

import jax
import jax.numpy as jnp
from jax import lax
from jax.experimental import pallas as pl
from jax.experimental.pallas import tpu as pltpu
from jax.sharding import PartitionSpec as P

CL_GROUP = 4
CAP = 16
LIFT = 4.0
LABEL_ROWS = 16
F32, BF16, I32 = jnp.float32, jnp.bfloat16, jnp.int32
NT = (((1,), (1,)), ((), ()))
NN = (((1,), (0,)), ((), ()))
TN = (((0,), (0,)), ((), ()))
VMEM = pl.BlockSpec(memory_space=pltpu.VMEM)
SMEM = pl.BlockSpec(memory_space=pltpu.SMEM)


def dot(a, b, dims):
    return lax.dot_general(a, b, dims, preferred_element_type=F32)


def iota(shape, dim):
    return lax.broadcasted_iota(I32, shape, dim)


def one_hot(condition):
    return condition.astype(F32).astype(BF16)


def call(kernel, out_shape, in_specs, flops, size):
    return pl.pallas_call(
        kernel,
        out_shape=out_shape,
        in_specs=in_specs,
        out_specs=jax.tree.map(lambda _: VMEM, out_shape),
        compiler_params=pltpu.CompilerParams(vmem_limit_bytes=24 * 1024 * 1024),
        cost_estimate=pl.CostEstimate(flops=flops, bytes_accessed=size, transcendentals=0),
    )


def place_kernel(offset_ref, rows_ref, labels_ref, out_ref, slot_ref):
    docs, width = rows_ref.shape
    groups, tall, lanes = out_ref.shape
    labels = labels_ref[...]
    owner = labels >> 2
    mine = iota((groups, docs), 0) == owner
    before = one_hot(iota((docs, docs), 0) < iota((docs, docs), 1))
    earlier = dot(one_hot(mine), before, NN)
    rank = jnp.sum(jnp.where(mine, earlier, 0.0), axis=0, keepdims=True).astype(I32)
    slot = owner * CAP + rank
    slot_ref[...] = slot
    values = rows_ref[...].astype(F32)
    mean = jnp.mean(values * values, axis=1, keepdims=True)
    unit = (values * lax.rsqrt(mean + 1e-06) / math.sqrt(width)).astype(BF16)
    pick = one_hot(iota((groups * CAP, docs), 0) == slot)
    step = 2 * lanes
    for first in range(0, width, step):
        placed = dot(pick, unit[:, first : first + step], NN).astype(BF16)
        for half in range(2):
            k = first // lanes + half
            part = placed[:, half * lanes : (half + 1) * lanes]
            out_ref[:, k * CAP : (k + 1) * CAP, :] = part.reshape(groups, CAP, lanes)
    below = tall - CAP * width // lanes
    index = iota((groups * below, docs), 0)
    cluster = index & (below - 1)
    wanted = (labels == (index >> 3) * CL_GROUP + cluster) & (cluster < CL_GROUP)
    lane = one_hot(iota((lanes, docs), 0) == rank + offset_ref[0])
    flags = dot(one_hot(wanted), lane, NT).astype(BF16)
    out_ref[:, tall - below :, :] = flags.reshape(groups, below, lanes)


def compact_kernel(capacity, in_ref, out_ref, position_ref):
    groups, tall, lanes = in_ref.shape
    width = out_ref.shape[1]
    count = width // lanes
    slots = groups * CAP
    below = tall - CAP * count
    labels = in_ref[:, tall - below :, :].astype(F32)
    per = lanes // CAP
    labels = jnp.sum(labels.reshape(groups // per, per, below, lanes), axis=1)
    labels = jnp.concatenate([labels[i] for i in range(groups // per)], axis=1)
    valid = jnp.sum(labels, axis=0, keepdims=True)
    before = one_hot(iota((slots, slots), 0) < iota((slots, slots), 1))
    rank = dot(jnp.broadcast_to(valid, (8, slots)).astype(BF16), before, NN)[:1]
    position = jnp.where(valid > 0.5, rank.astype(I32), -1)
    position_ref[...] = position
    total = jnp.sum(valid, axis=1, keepdims=True)
    over = jnp.broadcast_to(jnp.where(total > capacity + 0.5, 1.0, 0.0), (below, lanes))
    pick = one_hot(iota((capacity, slots), 0) == position)
    for k in range(count):
        part = in_ref[:, k * CAP : (k + 1) * CAP, :].reshape(slots, lanes)
        out_ref[:capacity, k * lanes : (k + 1) * lanes] = dot(pick, part, NN).astype(BF16)
    marks = dot(labels.astype(BF16), pick, NT).astype(BF16)
    marks = jnp.concatenate([marks, jnp.zeros((below, width - capacity), BF16)], axis=1)
    flag = jnp.concatenate([jnp.zeros((below, width - lanes), F32), over], axis=1).astype(BF16)
    out_ref[capacity:, :] = jnp.concatenate([marks, flag], axis=0)


def best_of(ref, others, capacity, skip_self=False):
    rows = ref[:capacity, :]
    marks = (ref[capacity:, :capacity].astype(F32) * LIFT).astype(BF16)
    best = None
    for other in others:
        if isinstance(other, tuple):
            other = jnp.concatenate([part[...] for part in other], axis=0)
        scores = dot(other[:capacity, :], rows, NT) + dot(other[capacity:, :capacity], marks, TN)
        if skip_self and other is ref:
            same = iota((capacity, capacity), 0) == iota((capacity, capacity), 1)
            scores = jnp.where(same, -9.0, scores)
        column = jnp.max(scores, axis=0, keepdims=True)
        best = column if best is None else jnp.maximum(best, column)
    return best


def near_kernel(
    capacity, own_ref, twin_ref, a_ref, a_twin_ref, b_ref, b_twin_ref, position_ref, out_ref, column_ref
):
    others = (own_ref, twin_ref, a_ref, a_twin_ref, b_ref, b_twin_ref)
    out_ref[...] = best_of(own_ref, others, capacity, skip_self=True)
    slots = position_ref.shape[1]
    diagonal = iota((slots, slots), 0) == iota((slots, slots), 1)
    column = jnp.max(jnp.where(diagonal, position_ref[...], -1), axis=1, keepdims=True)
    column_ref[...] = jnp.broadcast_to(column, column_ref.shape)


def middle_kernel(capacity, a2_ref, own_ref, twin_ref, b_ref, b_twin_ref, out_ref):
    out_ref[...] = best_of(a2_ref, (own_ref, twin_ref, b_ref, b_twin_ref), capacity)


def told_row(best, seen, refs, wide):
    flags = seen
    for ref in refs:
        flag = ref[ref.shape[0] - LABEL_ROWS :, ref.shape[1] - 128 :].astype(F32)
        flags = jnp.maximum(flags, jnp.max(flag, axis=0, keepdims=True))
    return jnp.concatenate([best, flags[:, : wide - best.shape[1]]], axis=1)


def a2_kernel(
    capacity, a2_best, a2_ref, own_ref, twin_ref, b_ref, b_twin_ref, twin_0, twin_1, out_ref
):
    best = jnp.maximum(a2_best[...], best_of(a2_ref, ((twin_0, twin_1),), capacity))
    blocks = (a2_ref, own_ref, twin_ref, b_ref, b_twin_ref, twin_1)
    out_ref[...] = told_row(best, jnp.zeros((1, 128), F32), blocks, out_ref.shape[1])


def b2_kernel(capacity, seen_ref, b2_ref, own_ref, twin_ref, a_ref, a_twin_ref, a2_ref, out_ref):
    seen = jnp.broadcast_to(seen_ref[...][:, capacity : capacity + 1], (1, 128))
    blocks = (own_ref, twin_ref, a_ref, a_twin_ref, a2_ref)
    best = best_of(b2_ref, blocks, capacity)
    out_ref[...] = told_row(best, seen, (b2_ref, *blocks), out_ref.shape[1])


def answer_kernel(capacity, near_ref, seen_ref, told_a, told_b, position_ref, out_ref):
    slots = position_ref.shape[0]
    groups, lanes = out_ref.shape
    told = jnp.maximum(told_a[...], told_b[...])
    over = jnp.maximum(told, seen_ref[...])[:, capacity : capacity + 1]
    best = jnp.maximum(jnp.maximum(near_ref[...], told[:, :capacity]) - LIFT, -1.0)
    hit = iota((slots, capacity), 1) == position_ref[:, :1]
    values = jnp.max(jnp.where(hit, best, -1.0), axis=1, keepdims=True)
    values = jnp.broadcast_to(values, (slots, lanes)).reshape(groups, CAP, lanes)
    same = iota((groups, CAP, lanes), 1) == iota((groups, CAP, lanes), 2)
    answers = jnp.max(jnp.where(same, values, -1.0), axis=1)
    out_ref[...] = jnp.where(iota((groups, lanes), 1) == CAP, over, answers)


def home_kernel(slot_ref, answers_ref, out_ref, over_ref):
    groups, lanes = answers_ref.shape
    docs = slot_ref.shape[1]
    answers = answers_ref[...]
    over = jnp.max(answers[:, CAP : CAP + 1], axis=0, keepdims=True)
    over_ref[...] = jnp.broadcast_to((over > 0.5).astype(I32), over_ref.shape)
    spread = jnp.broadcast_to(answers[:, None, :], (groups, CAP, lanes))
    same = iota((groups, CAP, lanes), 1) == iota((groups, CAP, lanes), 2)
    column = jnp.max(jnp.where(same, spread, -1.0), axis=2, keepdims=True)
    column = column.reshape(groups * CAP, 1)
    hit = iota((groups * CAP, docs), 0) == slot_ref[...]
    out_ref[...] = jnp.max(jnp.where(hit, column, -1.0), axis=0, keepdims=True)


def turn(step):
    size = lax.axis_size("narrow")
    return [(i, (i + 2 * (step if i % 2 == 0 else -step)) % size) for i in range(size)]


def nearest(received, slot, capacity):
    width = 1024
    groups, tall, lanes = received.shape
    slots = groups * CAP
    size = lax.axis_size("narrow")
    shape = jax.ShapeDtypeStruct
    block_bytes = 2 * (capacity + LABEL_ROWS) * width
    product = 2 * capacity * capacity * (width + 128)
    line = shape((1, capacity), F32)
    block, position = call(
        functools.partial(compact_kernel, capacity),
        (shape((capacity + LABEL_ROWS, width), BF16), shape((1, slots), I32)),
        [VMEM],
        2 * capacity * slots * width,
        received.size * 2 + block_bytes,
    )(received)

    def send(rows, pairs):
        return lax.ppermute(rows, "narrow", pairs)

    twins = [(i, i ^ 1) for i in range(size)]
    a = send(block, turn(-1))
    b = send(block, turn(1))
    twin = send(block, twins)
    a2 = send(a, turn(-1))
    b2 = send(b, turn(1))
    late_a, twin = lax.optimization_barrier((a, twin))
    b_twin = send(late_a, twins)
    a_twin = send(b, twins)
    half = (capacity + LABEL_ROWS) // 32 * 16
    b2_twin = send(a2[:half], twins), send(a2[half:], twins)
    told = shape((1, (capacity // 128 + 1) * 128), F32)
    a2_best = call(
        functools.partial(middle_kernel, capacity), line, [VMEM] * 5, 4 * product, 5 * block_bytes
    )(a2, block, twin, b, b_twin)
    to_a2 = call(
        functools.partial(a2_kernel, capacity), told, [VMEM] * 8, product, 2 * block_bytes
    )(a2_best, a2, block, twin, b, b_twin, *b2_twin)
    to_b2 = call(
        functools.partial(b2_kernel, capacity), told, [VMEM] * 7, 5 * product, 6 * block_bytes
    )(to_a2, b2, block, twin, a, a_twin, a2)
    near, column = call(
        functools.partial(near_kernel, capacity),
        (line, shape((slots, lanes), I32)),
        [VMEM] * 7,
        6 * product,
        6 * block_bytes,
    )(block, twin, a, a_twin, b, b_twin, position)
    told_a = send(to_a2, turn(2))
    told_b = send(to_b2, turn(-2))
    answers = call(
        functools.partial(answer_kernel, capacity),
        shape((groups, lanes), F32),
        [VMEM] * 5,
        slots * slots * 8,
        groups * lanes * 8,
    )(near, to_b2, told_a, told_b, column)
    answers = lax.all_to_all(answers, "wide", split_axis=0, concat_axis=0, tiled=True)
    return call(
        home_kernel,
        (shape(slot.shape, F32), shape((1, 128), I32)),
        [VMEM] * 2,
        slots * slot.shape[1] * 4,
        groups * lanes * 4,
    )(slot, answers)


def shards(embeddings, labels):
    docs, width = embeddings.shape
    groups = lax.axis_size("wide")
    lanes = 128
    tall = CAP * width // lanes + 8
    shape = jax.ShapeDtypeStruct
    offset = (lax.axis_index("wide") % (lanes // CAP) * CAP).astype(I32).reshape(1)
    outgoing, slot = call(
        place_kernel,
        (shape((groups, tall, lanes), BF16), shape((1, docs), I32)),
        [SMEM, VMEM, VMEM],
        2 * groups * CAP * docs * width,
        2 * docs * width + 2 * groups * tall * lanes,
    )(offset, embeddings, labels.reshape(1, docs))
    received = lax.all_to_all(outgoing, "wide", split_axis=0, concat_axis=0, tiled=True)
    quick, over = nearest(received, slot, 320)
    result = lax.cond(
        over[0, 0] > 0,
        lambda rows, places, unused: nearest(rows, places, groups * CAP)[0],
        lambda rows, places, done: done,
        received,
        slot,
        quick,
    )
    return result.reshape(docs)


def solution(mesh):
    in_specs = (P(("wide", "narrow"), None), P(("wide", "narrow")))
    out_specs = P(("wide", "narrow"))
    return jax.shard_map(shards, mesh=mesh, in_specs=in_specs, out_specs=out_specs, check_vma=False)
```

```python
import functools
import math

import jax
import jax.numpy as jnp
from jax import lax
from jax.experimental import pallas as pl
from jax.experimental.pallas import tpu as pltpu
from jax.sharding import PartitionSpec as P

CL_GROUP = 4
CAP = 16
LIFT = 4.0
LABEL_ROWS = 8
F32, BF16, I32 = jnp.float32, jnp.bfloat16, jnp.int32
NT = (((1,), (1,)), ((), ()))
NN = (((1,), (0,)), ((), ()))
TN = (((0,), (0,)), ((), ()))
VMEM = pl.BlockSpec(memory_space=pltpu.VMEM)
SMEM = pl.BlockSpec(memory_space=pltpu.SMEM)


def dot(a, b, dims):
    return lax.dot_general(a, b, dims, preferred_element_type=F32)


def iota(shape, dim):
    return lax.broadcasted_iota(I32, shape, dim)


def one_hot(condition):
    return condition.astype(F32).astype(BF16)


def call(kernel, out_shape, in_specs, flops, size):
    return pl.pallas_call(
        kernel,
        out_shape=out_shape,
        in_specs=in_specs,
        out_specs=jax.tree.map(lambda _: VMEM, out_shape),
        compiler_params=pltpu.CompilerParams(vmem_limit_bytes=24 * 1024 * 1024),
        cost_estimate=pl.CostEstimate(flops=flops, bytes_accessed=size, transcendentals=0),
    )


def place_kernel(offset_ref, rows_ref, labels_ref, out_ref, slot_ref):
    docs, width = rows_ref.shape
    groups, tall, lanes = out_ref.shape
    labels = labels_ref[...]
    owner = labels >> 2
    mine = iota((groups, docs), 0) == owner
    before = one_hot(iota((docs, docs), 0) < iota((docs, docs), 1))
    earlier = dot(one_hot(mine), before, NN)
    rank = jnp.sum(jnp.where(mine, earlier, 0.0), axis=0, keepdims=True).astype(I32)
    slot = owner * CAP + rank
    slot_ref[...] = slot
    values = rows_ref[...].astype(F32)
    mean = jnp.mean(values * values, axis=1, keepdims=True)
    unit = (values * lax.rsqrt(mean + 1e-06) / math.sqrt(width)).astype(BF16)
    pick = one_hot(iota((groups * CAP, docs), 0) == slot)
    step = 2 * lanes
    for first in range(0, width, step):
        placed = dot(pick, unit[:, first : first + step], NN).astype(BF16)
        for half in range(2):
            k = first // lanes + half
            part = placed[:, half * lanes : (half + 1) * lanes]
            out_ref[:, k * CAP : (k + 1) * CAP, :] = part.reshape(groups, CAP, lanes)
    below = tall - CAP * width // lanes
    index = iota((groups * below, docs), 0)
    cluster = index & (below - 1)
    wanted = (labels == (index >> 3) * CL_GROUP + cluster) & (cluster < CL_GROUP)
    lane = one_hot(iota((lanes, docs), 0) == rank + offset_ref[0])
    flags = dot(one_hot(wanted), lane, NT).astype(BF16)
    out_ref[:, tall - below :, :] = flags.reshape(groups, below, lanes)


def compact_kernel(capacity, in_ref, out_ref, position_ref):
    groups, tall, lanes = in_ref.shape
    width = out_ref.shape[1]
    count = width // lanes
    slots = groups * CAP
    below = tall - CAP * count
    labels = in_ref[:, tall - below :, :].astype(F32)
    per = lanes // CAP
    labels = jnp.sum(labels.reshape(groups // per, per, below, lanes), axis=1)
    labels = jnp.concatenate([labels[i] for i in range(groups // per)], axis=1)
    valid = jnp.sum(labels, axis=0, keepdims=True)
    before = one_hot(iota((slots, slots), 0) < iota((slots, slots), 1))
    rank = dot(jnp.broadcast_to(valid, (8, slots)).astype(BF16), before, NN)[:1]
    position = jnp.where(valid > 0.5, rank.astype(I32), -1)
    position_ref[...] = position
    total = jnp.sum(valid, axis=1, keepdims=True)
    over = jnp.broadcast_to(jnp.where(total > capacity + 0.5, 1.0, 0.0), (below, lanes))
    pick = one_hot(iota((capacity, slots), 0) == position)
    for k in range(count):
        part = in_ref[:, k * CAP : (k + 1) * CAP, :].reshape(slots, lanes)
        out_ref[:capacity, k * lanes : (k + 1) * lanes] = dot(pick, part, NN).astype(BF16)
    marks = dot(labels.astype(BF16), pick, NT).astype(BF16)
    gap = jnp.zeros((below, width - lanes - capacity), BF16)
    out_ref[capacity:, :] = jnp.concatenate([marks, gap, over.astype(BF16)], axis=1)


def best_of(ref, others, capacity, skip_self=False):
    rows = ref[:capacity, :]
    marks = (ref[capacity:, :capacity].astype(F32) * LIFT).astype(BF16)
    best = None
    for other in others:
        if isinstance(other, tuple):
            other = jnp.concatenate([part[...] for part in other], axis=0)
        scores = dot(other[:capacity, :], rows, NT) + dot(other[capacity:, :capacity], marks, TN)
        if skip_self and other is ref:
            same = iota((capacity, capacity), 0) == iota((capacity, capacity), 1)
            scores = jnp.where(same, -9.0, scores)
        column = jnp.max(scores, axis=0, keepdims=True)
        best = column if best is None else jnp.maximum(best, column)
    return best


def near_kernel(
    capacity, own_ref, twin_ref, a_ref, a_twin_ref, b_ref, b_twin_ref, position_ref, out_ref, column_ref
):
    others = (own_ref, twin_ref, a_ref, a_twin_ref, b_ref, b_twin_ref)
    out_ref[...] = best_of(own_ref, others, capacity, skip_self=True)
    slots = position_ref.shape[1]
    diagonal = iota((slots, slots), 0) == iota((slots, slots), 1)
    column = jnp.max(jnp.where(diagonal, position_ref[...], -1), axis=1, keepdims=True)
    column_ref[...] = jnp.broadcast_to(column, column_ref.shape)


def middle_kernel(capacity, a2_ref, own_ref, twin_ref, b_ref, b_twin_ref, out_ref):
    out_ref[...] = best_of(a2_ref, (own_ref, twin_ref, b_ref, b_twin_ref), capacity)


def told_row(best, seen, refs, wide):
    flags = seen
    for ref in refs:
        flag = ref[ref.shape[0] - LABEL_ROWS :, ref.shape[1] - 128 :].astype(F32)
        flags = jnp.maximum(flags, jnp.max(flag, axis=0, keepdims=True))
    return jnp.concatenate([best, flags[:, : wide - best.shape[1]]], axis=1)


def a2_kernel(
    capacity, a2_best, a2_ref, own_ref, twin_ref, b_ref, b_twin_ref, twin_0, twin_1, out_ref
):
    best = jnp.maximum(a2_best[...], best_of(a2_ref, ((twin_0, twin_1),), capacity))
    blocks = (a2_ref, own_ref, twin_ref, b_ref, b_twin_ref, twin_1)
    out_ref[...] = told_row(best, jnp.zeros((1, 128), F32), blocks, out_ref.shape[1])


def b2_kernel(capacity, seen_ref, b2_ref, own_ref, twin_ref, a_ref, a_twin_ref, a2_ref, out_ref):
    seen = jnp.broadcast_to(seen_ref[...][:, capacity : capacity + 1], (1, 128))
    blocks = (own_ref, twin_ref, a_ref, a_twin_ref, a2_ref)
    best = best_of(b2_ref, blocks, capacity)
    out_ref[...] = told_row(best, seen, (b2_ref, *blocks), out_ref.shape[1])


def answer_kernel(capacity, near_ref, seen_ref, told_a, told_b, position_ref, out_ref):
    slots = position_ref.shape[0]
    groups, lanes = out_ref.shape
    told = jnp.maximum(told_a[...], told_b[...])
    over = jnp.maximum(told, seen_ref[...])[:, capacity : capacity + 1]
    best = jnp.maximum(jnp.maximum(near_ref[...], told[:, :capacity]) - LIFT, -1.0)
    hit = iota((slots, capacity), 1) == position_ref[:, :1]
    values = jnp.max(jnp.where(hit, best, -1.0), axis=1, keepdims=True)
    values = jnp.broadcast_to(values, (slots, lanes)).reshape(groups, CAP, lanes)
    same = iota((groups, CAP, lanes), 1) == iota((groups, CAP, lanes), 2)
    answers = jnp.max(jnp.where(same, values, -1.0), axis=1)
    out_ref[...] = jnp.where(iota((groups, lanes), 1) == CAP, over, answers)


def home_kernel(slot_ref, answers_ref, out_ref, over_ref):
    groups, lanes = answers_ref.shape
    docs = slot_ref.shape[1]
    answers = answers_ref[...]
    over = jnp.max(answers[:, CAP : CAP + 1], axis=0, keepdims=True)
    over_ref[...] = jnp.broadcast_to((over > 0.5).astype(I32), over_ref.shape)
    spread = jnp.broadcast_to(answers[:, None, :], (groups, CAP, lanes))
    same = iota((groups, CAP, lanes), 1) == iota((groups, CAP, lanes), 2)
    column = jnp.max(jnp.where(same, spread, -1.0), axis=2, keepdims=True)
    column = column.reshape(groups * CAP, 1)
    hit = iota((groups * CAP, docs), 0) == slot_ref[...]
    out_ref[...] = jnp.max(jnp.where(hit, column, -1.0), axis=0, keepdims=True)


def turn(step):
    size = lax.axis_size("narrow")
    return [(i, (i + 2 * (step if i % 2 == 0 else -step)) % size) for i in range(size)]


def nearest(received, slot, capacity):
    width = 1024
    groups, tall, lanes = received.shape
    slots = groups * CAP
    size = lax.axis_size("narrow")
    shape = jax.ShapeDtypeStruct
    block_bytes = 2 * (capacity + LABEL_ROWS) * width
    product = 2 * capacity * capacity * (width + 128)
    line = shape((1, capacity), F32)
    block, position = call(
        functools.partial(compact_kernel, capacity),
        (shape((capacity + LABEL_ROWS, width), BF16), shape((1, slots), I32)),
        [VMEM],
        2 * capacity * slots * width,
        received.size * 2 + block_bytes,
    )(received)

    def send(rows, pairs):
        return lax.ppermute(rows, "narrow", pairs)

    twins = [(i, i ^ 1) for i in range(size)]
    a = send(block, turn(-1))
    b = send(block, turn(1))
    twin = send(block, twins)
    a2 = send(a, turn(-1))
    b2 = send(b, turn(1))
    late_a, twin = lax.optimization_barrier((a, twin))
    b_twin = send(late_a, twins)
    a_twin = send(b, twins)
    half = (capacity + LABEL_ROWS) // 32 * 16
    b2_twin = send(a2[:half], twins), send(a2[half:], twins)
    told = shape((1, (capacity // 128 + 1) * 128), F32)
    a2_best = call(
        functools.partial(middle_kernel, capacity), line, [VMEM] * 5, 4 * product, 5 * block_bytes
    )(a2, block, twin, b, b_twin)
    to_a2 = call(
        functools.partial(a2_kernel, capacity), told, [VMEM] * 8, product, 2 * block_bytes
    )(a2_best, a2, block, twin, b, b_twin, *b2_twin)
    to_b2 = call(
        functools.partial(b2_kernel, capacity), told, [VMEM] * 7, 5 * product, 6 * block_bytes
    )(to_a2, b2, block, twin, a, a_twin, a2)
    near, column = call(
        functools.partial(near_kernel, capacity),
        (line, shape((slots, lanes), I32)),
        [VMEM] * 7,
        6 * product,
        6 * block_bytes,
    )(block, twin, a, a_twin, b, b_twin, position)
    told_a = send(to_a2, turn(2))
    told_b = send(to_b2, turn(-2))
    answers = call(
        functools.partial(answer_kernel, capacity),
        shape((groups, lanes), F32),
        [VMEM] * 5,
        slots * slots * 8,
        groups * lanes * 8,
    )(near, to_b2, told_a, told_b, column)
    answers = lax.all_to_all(answers, "wide", split_axis=0, concat_axis=0, tiled=True)
    return call(
        home_kernel,
        (shape(slot.shape, F32), shape((1, 128), I32)),
        [VMEM] * 2,
        slots * slot.shape[1] * 4,
        groups * lanes * 4,
    )(slot, answers)


def shards(embeddings, labels):
    docs, width = embeddings.shape
    groups = lax.axis_size("wide")
    lanes = 128
    tall = CAP * width // lanes + 8
    shape = jax.ShapeDtypeStruct
    offset = (lax.axis_index("wide") % (lanes // CAP) * CAP).astype(I32).reshape(1)
    outgoing, slot = call(
        place_kernel,
        (shape((groups, tall, lanes), BF16), shape((1, docs), I32)),
        [SMEM, VMEM, VMEM],
        2 * groups * CAP * docs * width,
        2 * docs * width + 2 * groups * tall * lanes,
    )(offset, embeddings, labels.reshape(1, docs))
    received = lax.all_to_all(outgoing, "wide", split_axis=0, concat_axis=0, tiled=True)
    quick, over = nearest(received, slot, 320)
    result = lax.cond(
        over[0, 0] > 0,
        lambda rows, places, unused: nearest(rows, places, groups * CAP)[0],
        lambda rows, places, done: done,
        received,
        slot,
        quick,
    )
    return result.reshape(docs)


def solution(mesh):
    in_specs = (P(("wide", "narrow"), None), P(("wide", "narrow")))
    out_specs = P(("wide", "narrow"))
    return jax.shard_map(shards, mesh=mesh, in_specs=in_specs, out_specs=out_specs, check_vma=False)
```

```python
import functools
import math

import jax
import jax.numpy as jnp
from jax import lax
from jax.experimental import pallas as pl
from jax.experimental.pallas import tpu as pltpu
from jax.sharding import PartitionSpec as P

CL_GROUP = 4
CAP = 16
LIFT = 4.0
LABEL_ROWS = 8
F32, BF16, I32 = jnp.float32, jnp.bfloat16, jnp.int32
NT = (((1,), (1,)), ((), ()))
NN = (((1,), (0,)), ((), ()))
TN = (((0,), (0,)), ((), ()))
VMEM = pl.BlockSpec(memory_space=pltpu.VMEM)
SMEM = pl.BlockSpec(memory_space=pltpu.SMEM)


def dot(a, b, dims):
    return lax.dot_general(a, b, dims, preferred_element_type=F32)


def iota(shape, dim):
    return lax.broadcasted_iota(I32, shape, dim)


def one_hot(condition):
    return condition.astype(F32).astype(BF16)


def call(kernel, out_shape, in_specs, flops, size):
    return pl.pallas_call(
        kernel,
        out_shape=out_shape,
        in_specs=in_specs,
        out_specs=jax.tree.map(lambda _: VMEM, out_shape),
        compiler_params=pltpu.CompilerParams(vmem_limit_bytes=24 * 1024 * 1024),
        cost_estimate=pl.CostEstimate(flops=flops, bytes_accessed=size, transcendentals=0),
    )


def place_kernel(offset_ref, rows_ref, labels_ref, out_ref, slot_ref):
    docs, width = rows_ref.shape
    groups, tall, lanes = out_ref.shape
    labels = labels_ref[...]
    owner = labels >> 2
    mine = iota((groups, docs), 0) == owner
    before = one_hot(iota((docs, docs), 0) < iota((docs, docs), 1))
    earlier = dot(one_hot(mine), before, NN)
    rank = jnp.sum(jnp.where(mine, earlier, 0.0), axis=0, keepdims=True).astype(I32)
    slot = owner * CAP + rank
    slot_ref[...] = slot
    values = rows_ref[...].astype(F32)
    mean = jnp.mean(values * values, axis=1, keepdims=True)
    unit = (values * lax.rsqrt(mean + 1e-06) / math.sqrt(width)).astype(BF16)
    pick = one_hot(iota((groups * CAP, docs), 0) == slot)
    step = 2 * lanes
    for first in range(0, width, step):
        placed = dot(pick, unit[:, first : first + step], NN).astype(BF16)
        for half in range(2):
            k = first // lanes + half
            part = placed[:, half * lanes : (half + 1) * lanes]
            out_ref[:, k * CAP : (k + 1) * CAP, :] = part.reshape(groups, CAP, lanes)
    below = tall - CAP * width // lanes
    index = iota((groups * below, docs), 0)
    cluster = index & (below - 1)
    wanted = (labels == (index >> 3) * CL_GROUP + cluster) & (cluster < CL_GROUP)
    lane = one_hot(iota((lanes, docs), 0) == rank + offset_ref[0])
    flags = dot(one_hot(wanted), lane, NT).astype(BF16)
    out_ref[:, tall - below :, :] = flags.reshape(groups, below, lanes)


def compact_kernel(capacity, in_ref, out_ref, position_ref):
    groups, tall, lanes = in_ref.shape
    width = out_ref.shape[1]
    count = width // lanes
    slots = groups * CAP
    below = tall - CAP * count
    labels = in_ref[:, tall - below :, :].astype(F32)
    per = lanes // CAP
    labels = jnp.sum(labels.reshape(groups // per, per, below, lanes), axis=1)
    labels = jnp.concatenate([labels[i] for i in range(groups // per)], axis=1)
    valid = jnp.sum(labels, axis=0, keepdims=True)
    before = one_hot(iota((slots, slots), 0) < iota((slots, slots), 1))
    rank = dot(jnp.broadcast_to(valid, (8, slots)).astype(BF16), before, NN)[:1]
    position = jnp.where(valid > 0.5, rank.astype(I32), -1)
    position_ref[...] = position
    total = jnp.sum(valid, axis=1, keepdims=True)
    over = jnp.broadcast_to(jnp.where(total > capacity + 0.5, 1.0, 0.0), (below, lanes))
    pick = one_hot(iota((capacity, slots), 0) == position)
    for k in range(count):
        part = in_ref[:, k * CAP : (k + 1) * CAP, :].reshape(slots, lanes)
        out_ref[:capacity, k * lanes : (k + 1) * lanes] = dot(pick, part, NN).astype(BF16)
    marks = dot(labels.astype(BF16), pick, NT).astype(BF16)
    gap = jnp.zeros((below, width - lanes - capacity), BF16)
    out_ref[capacity:, :] = jnp.concatenate([marks, gap, over.astype(BF16)], axis=1)


def best_of(ref, others, capacity, skip_self=False):
    rows = ref[:capacity, :]
    marks = (ref[capacity:, :capacity].astype(F32) * LIFT).astype(BF16)
    best = None
    for other in others:
        if isinstance(other, tuple):
            other = jnp.concatenate([part[...] for part in other], axis=0)
        scores = dot(other[:capacity, :], rows, NT) + dot(other[capacity:, :capacity], marks, TN)
        if skip_self and other is ref:
            same = iota((capacity, capacity), 0) == iota((capacity, capacity), 1)
            scores = jnp.where(same, -9.0, scores)
        column = jnp.max(scores, axis=0, keepdims=True)
        best = column if best is None else jnp.maximum(best, column)
    return best


def near_kernel(
    capacity, own_ref, twin_ref, a_ref, a_twin_ref, b_ref, b_twin_ref, position_ref, out_ref, column_ref
):
    others = (own_ref, twin_ref, a_ref, a_twin_ref, b_ref, b_twin_ref)
    out_ref[...] = best_of(own_ref, others, capacity, skip_self=True)
    slots = position_ref.shape[1]
    diagonal = iota((slots, slots), 0) == iota((slots, slots), 1)
    column = jnp.max(jnp.where(diagonal, position_ref[...], -1), axis=1, keepdims=True)
    column_ref[...] = jnp.broadcast_to(column, column_ref.shape)


def middle_kernel(capacity, a2_ref, own_ref, twin_ref, b_ref, b_twin_ref, out_ref):
    out_ref[...] = best_of(a2_ref, (own_ref, twin_ref, b_ref, b_twin_ref), capacity)


def told_row(best, seen, refs, wide):
    flags = seen
    for ref in refs:
        flag = ref[ref.shape[0] - LABEL_ROWS :, ref.shape[1] - 128 :].astype(F32)
        flags = jnp.maximum(flags, jnp.max(flag, axis=0, keepdims=True))
    return jnp.concatenate([best, flags[:, : wide - best.shape[1]]], axis=1)


def a2_kernel(
    capacity, a2_best, a2_ref, own_ref, twin_ref, b_ref, b_twin_ref, twin_0, twin_1, out_ref
):
    best = jnp.maximum(a2_best[...], best_of(a2_ref, ((twin_0, twin_1),), capacity))
    blocks = (a2_ref, own_ref, twin_ref, b_ref, b_twin_ref, twin_1)
    out_ref[...] = told_row(best, jnp.zeros((1, 128), F32), blocks, out_ref.shape[1])


def b2_kernel(capacity, seen_ref, b2_ref, own_ref, twin_ref, a_ref, a_twin_ref, a2_ref, out_ref):
    seen = jnp.broadcast_to(seen_ref[...][:, capacity : capacity + 1], (1, 128))
    blocks = (own_ref, twin_ref, a_ref, a_twin_ref, a2_ref)
    best = best_of(b2_ref, blocks, capacity)
    out_ref[...] = told_row(best, seen, (b2_ref, *blocks), out_ref.shape[1])


def answer_kernel(capacity, near_ref, seen_ref, told_a, told_b, position_ref, out_ref):
    slots = position_ref.shape[0]
    groups, lanes = out_ref.shape
    told = jnp.maximum(told_a[...], told_b[...])
    over = jnp.maximum(told, seen_ref[...])[:, capacity : capacity + 1]
    best = jnp.maximum(jnp.maximum(near_ref[...], told[:, :capacity]) - LIFT, -1.0)
    wide = told.shape[1]
    best = jnp.concatenate([best, jnp.full((1, wide - capacity), -1.0, F32)], axis=1)
    values = jnp.full((slots, lanes), -1.0, F32)
    for first in range(0, wide, lanes):
        hit = iota((slots, lanes), 1) + first == position_ref[...]
        values = jnp.maximum(values, jnp.where(hit, best[:, first : first + lanes], -1.0))
    values = jnp.max(values, axis=1, keepdims=True)
    values = jnp.broadcast_to(values, (slots, lanes)).reshape(groups, CAP, lanes)
    same = iota((groups, CAP, lanes), 1) == iota((groups, CAP, lanes), 2)
    answers = jnp.max(jnp.where(same, values, -1.0), axis=1)
    out_ref[...] = jnp.where(iota((groups, lanes), 1) == CAP, over, answers)


def home_kernel(slot_ref, answers_ref, out_ref, over_ref):
    groups, lanes = answers_ref.shape
    docs = slot_ref.shape[1]
    answers = answers_ref[...]
    over = jnp.max(answers[:, CAP : CAP + 1], axis=0, keepdims=True)
    over_ref[...] = jnp.broadcast_to((over > 0.5).astype(I32), over_ref.shape)
    spread = jnp.broadcast_to(answers[:, None, :], (groups, CAP, lanes))
    same = iota((groups, CAP, lanes), 1) == iota((groups, CAP, lanes), 2)
    column = jnp.max(jnp.where(same, spread, -1.0), axis=2, keepdims=True)
    column = column.reshape(groups * CAP, 1)
    hit = iota((groups * CAP, docs), 0) == slot_ref[...]
    out_ref[...] = jnp.max(jnp.where(hit, column, -1.0), axis=0, keepdims=True)


def turn(step):
    size = lax.axis_size("narrow")
    return [(i, (i + 2 * (step if i % 2 == 0 else -step)) % size) for i in range(size)]


def nearest(received, slot, capacity):
    width = 1024
    groups, tall, lanes = received.shape
    slots = groups * CAP
    size = lax.axis_size("narrow")
    shape = jax.ShapeDtypeStruct
    block_bytes = 2 * (capacity + LABEL_ROWS) * width
    product = 2 * capacity * capacity * (width + 128)
    line = shape((1, capacity), F32)
    block, position = call(
        functools.partial(compact_kernel, capacity),
        (shape((capacity + LABEL_ROWS, width), BF16), shape((1, slots), I32)),
        [VMEM],
        2 * capacity * slots * width,
        received.size * 2 + block_bytes,
    )(received)

    def send(rows, pairs):
        return lax.ppermute(rows, "narrow", pairs)

    twins = [(i, i ^ 1) for i in range(size)]
    a = send(block, turn(-1))
    b = send(block, turn(1))
    twin = send(block, twins)
    a2 = send(a, turn(-1))
    b2 = send(b, turn(1))
    late_a, twin = lax.optimization_barrier((a, twin))
    b_twin = send(late_a, twins)
    a_twin = send(b, twins)
    half = (capacity + LABEL_ROWS) // 32 * 16
    b2_twin = send(a2[:half], twins), send(a2[half:], twins)
    told = shape((1, (capacity // 128 + 1) * 128), F32)
    a2_best = call(
        functools.partial(middle_kernel, capacity), line, [VMEM] * 5, 4 * product, 5 * block_bytes
    )(a2, block, twin, b, b_twin)
    to_a2 = call(
        functools.partial(a2_kernel, capacity), told, [VMEM] * 8, product, 2 * block_bytes
    )(a2_best, a2, block, twin, b, b_twin, *b2_twin)
    to_b2 = call(
        functools.partial(b2_kernel, capacity), told, [VMEM] * 7, 5 * product, 6 * block_bytes
    )(to_a2, b2, block, twin, a, a_twin, a2)
    near, column = call(
        functools.partial(near_kernel, capacity),
        (line, shape((slots, lanes), I32)),
        [VMEM] * 7,
        6 * product,
        6 * block_bytes,
    )(block, twin, a, a_twin, b, b_twin, position)
    told_a = send(to_a2, turn(2))
    told_b = send(to_b2, turn(-2))
    answers = call(
        functools.partial(answer_kernel, capacity),
        shape((groups, lanes), F32),
        [VMEM] * 5,
        slots * slots * 8,
        groups * lanes * 8,
    )(near, to_b2, told_a, told_b, column)
    answers = lax.all_to_all(answers, "wide", split_axis=0, concat_axis=0, tiled=True)
    return call(
        home_kernel,
        (shape(slot.shape, F32), shape((1, 128), I32)),
        [VMEM] * 2,
        slots * slot.shape[1] * 4,
        groups * lanes * 4,
    )(slot, answers)


def shards(embeddings, labels):
    docs, width = embeddings.shape
    groups = lax.axis_size("wide")
    lanes = 128
    tall = CAP * width // lanes + 8
    shape = jax.ShapeDtypeStruct
    offset = (lax.axis_index("wide") % (lanes // CAP) * CAP).astype(I32).reshape(1)
    outgoing, slot = call(
        place_kernel,
        (shape((groups, tall, lanes), BF16), shape((1, docs), I32)),
        [SMEM, VMEM, VMEM],
        2 * groups * CAP * docs * width,
        2 * docs * width + 2 * groups * tall * lanes,
    )(offset, embeddings, labels.reshape(1, docs))
    received = lax.all_to_all(outgoing, "wide", split_axis=0, concat_axis=0, tiled=True)
    quick, over = nearest(received, slot, 320)
    result = lax.cond(
        over[0, 0] > 0,
        lambda rows, places, unused: nearest(rows, places, groups * CAP)[0],
        lambda rows, places, done: done,
        received,
        slot,
        quick,
    )
    return result.reshape(docs)


def solution(mesh):
    in_specs = (P(("wide", "narrow"), None), P(("wide", "narrow")))
    out_specs = P(("wide", "narrow"))
    return jax.shard_map(shards, mesh=mesh, in_specs=in_specs, out_specs=out_specs, check_vma=False)
```
